32 devices in a mesh: ctx: 4 (over z), head: 8 (over y, x, core).
Axes of the slice: x: 2, y: 2, z: 4, core: 2. Of those that a mesh axis runs over, the one named last changes fastest.
Arguments:
- x_stream: bfloat16 [16384, 16384], P('ctx', 'head'), may hold values from -6 to 6
- gate_z: bfloat16 [16384, 16384], P('ctx', 'head'), as said below
- state_proj: bfloat16 [16384, 2048], P('ctx', 'head'), may hold values from -5 to 5
- dt_raw: float32 [16384, 256], P('ctx', 'head'), as said below
- dt_bias: float32 [256], P('head'), may hold values from -3 to -1
- a_log: float32 [256], P('head'), as said below
- skip_d: float32 [256], P('head'), may hold values from 0.5 to 1.5
- conv_x: bfloat16 [4, 16384], P(None, 'head'), may hold values from -3 to 3
- conv_proj: bfloat16 [4, 2048], P(None, 'head'), may hold values from -3 to 3
- norm_gain: float32 [16384], P('head'), may hold values from 0.5 to 1.5
Outputs:
- mixer_out: bfloat16 [16384, 16384], P('ctx', 'head')
The draws below stay inside these ranges and needn't reach their ends.
Inputs may be any that keep to these rules, and one draw needn't show every extreme that they name: gate_z is a bounded normal draw whose scale varies by column. dt_raw is bounded; its level varies over blocks of 4096 tokens and heads. a_log is finite.
All inputs are finite; a program needn't handle non-finite values.
Results may differ from the reference program's by a relative error of at most 0.0085.
Values may be sent and summed in bfloat16 or wider, within the bound.
A program may use at most 256 MiB of HBM per device.

```python
import math
import jax
import jax.numpy as jnp
from jax import lax

HEADS = 256
HEADDIM = 64
STATE = 128
GROUPS = 8
KCONV = 4
BLOCK_LEN = 128
TOK_DEV = 4096
TOKENS = 16384


def draw_gate_z(key, part):
    per_group = HEADS // GROUPS
    column = (jnp.arange(HEADS * HEADDIM) // HEADDIM % per_group).astype(jnp.float32)
    noise_part = jax.random.truncated_normal(key, -5.0, 5.0, (TOKENS, HEADS * HEADDIM), jnp.float32)
    rising = 0.5 + column / (per_group - 1.0)
    col_scale = rising
    return (noise_part * col_scale).astype(jnp.bfloat16)


def draw_dt_raw(key, part):
    blocks = TOKENS // TOK_DEV
    levels = jax.random.uniform(jax.random.fold_in(key, 11), (blocks, HEADS), jnp.float32, -0.7, 0.7)
    noise_part = 0.5 * jax.random.truncated_normal(key, -4.0, 4.0, (TOKENS, HEADS), jnp.float32)
    return noise_part + jnp.repeat(levels, TOK_DEV, axis=0)


def draw_a_log(key, part):
    typical_step = 0.127
    slow_rate = jnp.exp(jax.random.uniform(jax.random.fold_in(key, 3), (HEADS,), jnp.float32, math.log(0.3), math.log(2.0))) / TOKENS
    fast_rate = jnp.exp(jax.random.uniform(jax.random.fold_in(key, 5), (HEADS,), jnp.float32, math.log(0.02), math.log(0.06)))
    share = 0.5
    slow_mask = jax.random.uniform(jax.random.fold_in(key, 9), (HEADS,), jnp.float32) < share
    rate_per_token = jnp.where(slow_mask, slow_rate, fast_rate)
    return jnp.log(rate_per_token / typical_step)


def steps_of(key, extent, shards, smallest, high):
    factor_of, own = 1.0, jax.random.fold_in(key, 6)
    for axis_at, parts in shards:
        steps = jnp.exp(jax.random.uniform(jax.random.fold_in(own, axis_at), (parts,), jnp.float32, smallest / len(shards), high / len(shards)))
        factor_of = factor_of * jnp.repeat(steps, extent[axis_at] // parts).reshape([-1 if axis == axis_at else 1 for axis in range(len(extent))])
    return factor_of


def noise(stream_key, dims, deviation, reach, pieces=(), kind=jnp.bfloat16):
    array = jax.random.normal(stream_key, dims, jnp.float32) * deviation
    if len(pieces) > 0:
        array = steps_of(stream_key, dims, pieces, -0.22, 0.18) * array
    return jnp.clip(array, min=-reach, max=reach).astype(kind)


def setup_inputs(seed: int = 0) -> dict:
    keys = jax.random.split(jax.random.key(seed), 11)
    return {
        "x_stream": noise(keys[0], (TOKENS, HEADS * HEADDIM), 1.0, 6.0, ((0, 4), (1, 8))),
        "gate_z": draw_gate_z(jax.random.fold_in(keys[10], 71), 0),
        "state_proj": noise(keys[2], (TOKENS, 2 * GROUPS * STATE), 0.35, 5.0, ((0, 4), (1, 8))),
        "dt_raw": draw_dt_raw(jax.random.fold_in(keys[10], 71), 0),
        "dt_bias": jnp.clip(-3.0 + 2.0 * jax.random.uniform(keys[4], (HEADS,), jnp.float32) ** steps_of(keys[4], (HEADS,), ((0, 8),), -0.2, 0.2), -3.0, -1.0),
        "a_log": draw_a_log(jax.random.fold_in(keys[10], 71), 0),
        "skip_d": jnp.clip(0.5 + 1.0 * jax.random.uniform(keys[6], (HEADS,), jnp.float32) ** steps_of(keys[6], (HEADS,), ((0, 8),), -0.2, 0.2), 0.5, 1.5),
        "conv_x": noise(keys[7], (KCONV, HEADS * HEADDIM), KCONV ** -0.5, 3.0, ((1, 8),)),
        "conv_proj": noise(keys[8], (KCONV, 2 * GROUPS * STATE), KCONV ** -0.5, 3.0, ((1, 8),)),
        "norm_gain": jnp.clip(1.0 + 0.1 * jax.random.normal(keys[9], (HEADS * HEADDIM,), jnp.float32), 0.5, 1.5),
    }


def conv_silu(sequence, edge_rows, weight):
    kernel_len = weight.shape[0]
    length = sequence.shape[0]
    padded = jnp.concatenate([edge_rows, sequence], axis=0).astype(jnp.float32)
    weight_wide = weight.astype(jnp.float32)
    total = jnp.zeros(sequence.shape, jnp.float32)
    for offset in range(kernel_len):
        total = total + weight_wide[offset] * padded[offset:offset + length]
    return jax.nn.silu(total).astype(jnp.bfloat16)

def block_scan(x_blocks, b_blocks, c_blocks, step_size, log_decay, initial):
    highest = lax.Precision.HIGHEST
    running = jnp.cumsum(jnp.swapaxes(log_decay, 1, 2), axis=2)
    step_heads = jnp.swapaxes(step_size, 1, 2)
    b_wide = b_blocks.astype(jnp.float32)
    c_wide = c_blocks.astype(jnp.float32)
    x_wide = x_blocks.astype(jnp.float32)
    gram_matrix = jnp.einsum('ctn,csn->cts', c_wide, b_wide, precision=highest)
    block_len = running.shape[2]
    row_ids = jnp.arange(block_len)[:, None]
    col_ids = jnp.arange(block_len)[None, :]
    causal_mask = row_ids >= col_ids
    log_gaps = running[:, :, :, None] - running[:, :, None, :]
    decay_matrix = jnp.where(causal_mask, jnp.exp(jnp.where(causal_mask, log_gaps, 0.0)), 0.0)
    weights = (gram_matrix[:, None] * decay_matrix * step_heads[:, :, None, :]).astype(jnp.bfloat16)
    intra_out = jnp.einsum('chts,cshp->cthp', weights.astype(jnp.float32), x_wide, precision=highest)
    block_total = running[:, :, -1]
    state_weight = jnp.exp(block_total[:, :, None] - running) * step_heads
    weighted = (x_wide * jnp.swapaxes(state_weight, 1, 2)[..., None]).astype(jnp.bfloat16)
    states = jnp.einsum('cshp,csn->chpn', weighted.astype(jnp.float32), b_wide, precision=highest)

    def advance(state_now, inputs):
        factor, addend = inputs
        return (factor[:, None, None] * state_now + addend, state_now)
    final_state, entering = lax.scan(advance, initial, (jnp.exp(block_total), states))
    inter_out = jnp.exp(jnp.swapaxes(running, 1, 2))[..., None] * jnp.einsum('ctn,chpn->cthp', c_wide, entering, precision=highest)
    return (intra_out + inter_out, final_state, block_total, running)

def reference(x_stream, gate_z, state_proj, dt_raw, dt_bias, a_log, skip_d, conv_x, conv_proj, norm_gain):
    kernel_len = conv_x.shape[0]
    proj_conv = conv_silu(state_proj, jnp.zeros((kernel_len - 1, state_proj.shape[1]), jnp.bfloat16), conv_proj)
    step_size = jax.nn.softplus(dt_raw + dt_bias)
    log_decay = step_size * -jnp.exp(a_log)
    per_group = HEADS // GROUPS
    blocks = TOKENS // BLOCK_LEN
    gains = norm_gain.reshape(HEADS, HEADDIM)

    def group_out(group_id):
        own_cols = lax.dynamic_slice_in_dim(proj_conv, group_id * 2 * STATE, 2 * STATE, 1)
        b_blocks = own_cols[:, :STATE].reshape(blocks, BLOCK_LEN, STATE)
        c_blocks = own_cols[:, STATE:].reshape(blocks, BLOCK_LEN, STATE)

        def head_out(head_local):
            head_id = group_id * per_group + head_local
            x_head = lax.dynamic_slice_in_dim(x_stream, head_id * HEADDIM, HEADDIM, 1)
            w_head = lax.dynamic_slice_in_dim(conv_x, head_id * HEADDIM, HEADDIM, 1)
            x_conv = conv_silu(x_head, jnp.zeros((kernel_len - 1, HEADDIM), jnp.bfloat16), w_head)
            step_head = lax.dynamic_slice_in_dim(step_size, head_id, 1, 1).reshape(blocks, BLOCK_LEN, 1)
            decay_head = lax.dynamic_slice_in_dim(log_decay, head_id, 1, 1).reshape(blocks, BLOCK_LEN, 1)
            mixed, final_state, block_total, running = block_scan(x_conv.reshape(blocks, BLOCK_LEN, 1, HEADDIM), b_blocks, c_blocks, step_head, decay_head, jnp.zeros((1, HEADDIM, STATE), jnp.float32))
            skip_head = lax.dynamic_slice_in_dim(skip_d, head_id, 1, 0)
            mixed = mixed.reshape(TOKENS, HEADDIM) + skip_head * x_conv.astype(jnp.float32)
            z_head = lax.dynamic_slice_in_dim(gate_z, head_id * HEADDIM, HEADDIM, 1).astype(jnp.float32)
            return mixed * jax.nn.silu(z_head)
        gated_out = lax.map(head_out, jnp.arange(per_group, dtype=jnp.int32))
        mean_square = lax.optimization_barrier(jnp.mean(gated_out * gated_out, axis=(0, 2)))
        gain_group = lax.dynamic_slice_in_dim(gains, group_id * per_group, per_group, 0)
        normed = gated_out * lax.rsqrt(mean_square + 1e-05)[None, :, None] * gain_group[:, None, :]
        return normed.astype(jnp.bfloat16)
    normed = lax.map(group_out, jnp.arange(GROUPS, dtype=jnp.int32))
    return jnp.transpose(normed, (2, 0, 1, 3)).reshape(TOKENS, HEADS * HEADDIM)
```

```python
import functools

import jax
import jax.numpy as jnp
from jax import lax
from jax.experimental import pallas as pl
from jax.experimental.pallas import tpu as pltpu
from jax.sharding import PartitionSpec as P

HEADS = 256
STATE = 128
GROUPS = 8
BLOCK_LEN = 128
LANES = 128
CHUNK = 256
PIECES = 4
LOG2E = 1.4426950408889634


def passed_along(x, axis, by):
    count = lax.axis_size(axis)
    pairs = [(i, i + by) for i in range(count) if 0 <= i + by < count]
    return lax.ppermute(x, axis, pairs)


def swapped(value, axis, bit):
    mask = 2**bit
    pairs = [(source, source ^ mask) for source in range(lax.axis_size(axis))]
    return lax.ppermute(value, axis, pairs)


def conv_silu(sequence, edge_rows, weight):
    kernel_len = weight.shape[0]
    length = sequence.shape[0]
    padded = jnp.concatenate([edge_rows, sequence], axis=0).astype(jnp.float32)
    weight_wide = weight.astype(jnp.float32)
    total = jnp.zeros(sequence.shape, jnp.float32)
    for offset in range(kernel_len):
        total = total + weight_wide[offset] * padded[offset : offset + length]
    return jax.nn.silu(total).astype(jnp.bfloat16)


def join_pair(mine, other, upper):
    return jnp.where(
        upper, jnp.concatenate([other, mine], axis=1), jnp.concatenate([mine, other], axis=1)
    )


def dot(a, b):
    return jnp.dot(a, b, preferred_element_type=jnp.float32)


def two_terms(values):
    high = values.astype(jnp.bfloat16)
    low = (values - high.astype(jnp.float32)).astype(jnp.bfloat16)
    return jnp.concatenate([high, low], axis=1)


def state_kernel(
    x_ref, edge_ref, taps_ref, b_ref, vals_ref, spread_ref, decay_ref,
    conv_ref, entering_ref, final_ref, wide, state,
):
    step = pl.program_id(0)
    channels = x_ref.shape[1]
    columns = channels // LANES

    @pl.when(step == 0)
    def _():
        state[...] = jnp.zeros_like(state)
        for j in range(columns):
            wide[j, 0:8, :] = edge_ref[:, j * LANES : (j + 1) * LANES]

    @pl.when(step > 0)
    def _():
        for j in range(columns):
            wide[j, 0:8, :] = wide[j, BLOCK_LEN : BLOCK_LEN + 8, :]

    terms = two_terms(vals_ref[...])
    b_turned = b_ref[...].astype(jnp.float32).T.astype(jnp.bfloat16)
    for chunk in range(channels // CHUNK):
        cols = slice(chunk * CHUNK, (chunk + 1) * CHUNK)
        scale = dot(terms, spread_ref[:, cols])
        parts = []
        for sub in range(CHUNK // LANES):
            j = chunk * (CHUNK // LANES) + sub
            lanes = slice(j * LANES, (j + 1) * LANES)
            now = x_ref[:, lanes].astype(jnp.float32)
            wide[j, 8:, :] = now
            half = taps_ref[3:4, lanes] * now
            for k in range(3):
                half = half + taps_ref[k : k + 1, lanes] * wide[j, 5 + k : 5 + k + BLOCK_LEN, :]
            active = half + half * jnp.tanh(half)
            conv_ref[:, lanes] = active.astype(jnp.bfloat16)
            part = active * scale[:, sub * LANES : (sub + 1) * LANES]
            parts.append(part.astype(jnp.bfloat16))
        added = dot(b_turned, jnp.concatenate(parts, axis=1))
        held = state[:, cols]
        entering_ref[0, :, cols] = held.astype(jnp.bfloat16)
        state[:, cols] = held * decay_ref[0, :, cols] + added

    @pl.when(step == pl.num_programs(0) - 1)
    def _():
        final_ref[...] = state[...]


def chain_kernel(final_ref, decay_ref, out_ref, sent, got, send_sem, recv_sem):
    pos = lax.axis_index("ctx")
    count = lax.axis_size("ctx")
    rows = final_ref.shape[0] // PIECES
    barrier = pltpu.get_barrier_semaphore()

    @pl.when(pos > 0)
    def _():
        pl.semaphore_signal(
            barrier, inc=1, device_id={"ctx": lax.rem(pos + count - 1, count)},
            device_id_type=pl.DeviceIdType.MESH,
        )

    @pl.when(pos < count - 1)
    def _():
        pl.semaphore_wait(barrier, 1)

    def copy(piece):
        return pltpu.make_async_remote_copy(
            src_ref=sent.at[piece],
            dst_ref=got.at[piece],
            send_sem=send_sem.at[piece],
            recv_sem=recv_sem.at[piece],
            device_id={"ctx": lax.rem(pos + 1, count)},
            device_id_type=pl.DeviceIdType.MESH,
        )

    for piece in range(PIECES):
        at = slice(piece * rows, (piece + 1) * rows)

        @pl.when(pos == 0)
        def _():
            out_ref[at, :] = jnp.zeros((rows, out_ref.shape[1]), out_ref.dtype)
            sent[piece] = final_ref[at, :].astype(jnp.bfloat16)

        @pl.when(pos > 0)
        def _():
            copy(piece).wait_recv()
            before = got[piece]
            out_ref[at, :] = before
            sent[piece] = (
                final_ref[at, :] + decay_ref[...] * before.astype(jnp.float32)
            ).astype(jnp.bfloat16)

        @pl.when(pos < count - 1)
        def _():
            copy(piece).start()

    for piece in range(PIECES):

        @pl.when(pos < count - 1)
        def _():
            copy(piece).wait_send()


def mix_kernel(
    whole_group, conv_ref, gate_ref, bc_ref, vals_ref, run_ref, run_rows_ref, entering_ref,
    start_ref, before_ref, spread_step_ref, spread_decay_ref, skip_ref, gain_ref,
    *rest,
):
    if whole_group:
        out_ref, gated = rest
    else:
        gated, squares_ref = rest
    channels = conv_ref.shape[1]
    head_size = channels // run_rows_ref.shape[1]
    pair = LANES // head_size
    terms = two_terms(vals_ref[...])
    b_block = bc_ref[:, :STATE]
    c_block = bc_ref[:, STATE:]
    gram = lax.dot_general(
        c_block, b_block, (((1,), (1,)), ((), ())), preferred_element_type=jnp.float32
    )
    rows = lax.broadcasted_iota(jnp.int32, (BLOCK_LEN, BLOCK_LEN), 0)
    cols = lax.broadcasted_iota(jnp.int32, (BLOCK_LEN, BLOCK_LEN), 1)
    gram = jnp.where(rows >= cols, gram, 0.0)
    lane_head = cols // head_size
    squares = jnp.zeros((BLOCK_LEN, LANES), jnp.float32)
    for chunk in range(channels // CHUNK):
        at = slice(chunk * CHUNK, (chunk + 1) * CHUNK)
        step_wide = dot(terms, spread_step_ref[:, at])
        decay_wide = dot(terms, spread_decay_ref[:, at])
        held = entering_ref[0, :, at].astype(jnp.float32) + start_ref[0, :, at] * before_ref[
            :, at
        ].astype(jnp.float32)
        carried = decay_wide * dot(c_block, held.astype(jnp.bfloat16))
        for sub in range(CHUNK // LANES):
            j = chunk * (CHUNK // LANES) + sub
            here = slice(sub * LANES, (sub + 1) * LANES)
            lanes = slice(j * LANES, (j + 1) * LANES)
            x_wide = conv_ref[:, lanes].astype(jnp.float32)
            stepped = x_wide * step_wide[:, here]
            left, right = [], []
            for part in range(pair):
                head = j * pair + part
                gap = run_ref[:, head : head + 1] - run_rows_ref[0, head : head + 1, :]
                weights = gram * jnp.exp2(jnp.minimum(gap, 0.0))
                left.append(weights.astype(jnp.bfloat16))
                right.append(jnp.where(lane_head == part, stepped, 0.0).astype(jnp.bfloat16))
            intra = dot(jnp.concatenate(left, axis=1), jnp.concatenate(right, axis=0))
            mixed = intra + carried[:, here] + skip_ref[:, lanes] * x_wide
            half = 0.5 * gate_ref[:, lanes].astype(jnp.float32)
            value = mixed * (half + half * jnp.tanh(half))
            squares = squares + value * value
            gated[:, lanes] = value
    total = jnp.sum(squares, axis=1, keepdims=True)
    if whole_group:
        factor = lax.rsqrt(total * (1.0 / channels) + 1e-05)
        for j in range(channels // LANES):
            lanes = slice(j * LANES, (j + 1) * LANES)
            out_ref[:, lanes] = (gated[:, lanes] * factor * gain_ref[:, lanes]).astype(
                jnp.bfloat16
            )
    else:
        squares_ref[...] = jnp.broadcast_to(total, squares_ref.shape)


def on_device(
    x_stream, gate_z, state_proj, dt_raw, dt_bias, a_log, skip_d, conv_x, conv_proj, norm_gain
):
    highest = lax.Precision.HIGHEST
    f32, bf16 = jnp.float32, jnp.bfloat16
    kernel_len = conv_x.shape[0]
    tokens_here = x_stream.shape[0]
    heads_here = dt_raw.shape[1]
    channels = x_stream.shape[1]
    head_size = channels // heads_here
    head_pos = lax.axis_index("head")
    group_devices = lax.axis_size("head") // GROUPS
    group_levels = group_devices.bit_length() - 1
    whole_group = group_devices == 1
    blocks = tokens_here // BLOCK_LEN
    edge_start = tokens_here - kernel_len + 1
    edge_x, edge_proj = passed_along(
        (x_stream[edge_start:], state_proj[edge_start:]), "ctx", 1
    )
    own_cols = conv_silu(state_proj, edge_proj, conv_proj)
    for level in range(group_levels):
        upper = head_pos >> level & 1 == 1
        other_cols = swapped(own_cols, "head", level)
        own_cols = join_pair(own_cols, other_cols, upper)

    step_size = jax.nn.softplus(dt_raw + dt_bias)
    log_decay = (step_size * -jnp.exp(a_log)).reshape(blocks, BLOCK_LEN, heads_here)
    lower = jnp.tril(jnp.ones((BLOCK_LEN, BLOCK_LEN), f32))
    running = jnp.einsum("ts,bsh->bth", lower, log_decay, precision=highest)
    totals = running[:, -1]
    starts = jnp.cumsum(totals, axis=0) - totals
    step_blocks = step_size.reshape(blocks, BLOCK_LEN, heads_here)
    kinds = [
        step_blocks,
        jnp.exp(running),
        jnp.exp(totals[:, None] - running) * step_blocks,
    ]
    vals = jnp.concatenate(kinds, axis=2)
    vals = jnp.pad(vals, ((0, 0), (0, 0), (0, LANES - vals.shape[2])))
    vals = vals.reshape(tokens_here, LANES)
    run_scaled = running * LOG2E
    run_rows = jnp.swapaxes(run_scaled, 1, 2)
    run_scaled = run_scaled.reshape(tokens_here, heads_here)

    def per_channel(values):
        return jnp.repeat(values, head_size, axis=-1)[..., None, :]

    def spread(kind):
        row = jnp.arange(2 * LANES)[:, None] % LANES
        col = jnp.arange(channels)[None, :] // head_size
        return (row == col + kind * heads_here).astype(bf16)

    edge_wide = jnp.pad(edge_x.astype(f32), ((8 - kernel_len + 1, 0), (0, 0)))
    taps = jnp.pad(0.5 * conv_x.astype(f32), ((0, 8 - kernel_len), (0, 0)))

    token_block = pl.BlockSpec((BLOCK_LEN, channels), lambda b: (b, 0))
    vals_block = pl.BlockSpec((BLOCK_LEN, LANES), lambda b: (b, 0))
    row_block = pl.BlockSpec((1, 1, channels), lambda b: (b, 0, 0))
    state_block = pl.BlockSpec((1, STATE, channels), lambda b: (b, 0, 0))

    def fixed(rows):
        return pl.BlockSpec((rows, channels), lambda b: (0, 0))

    limit = pltpu.CompilerParams(
        vmem_limit_bytes=40 * 2**20, dimension_semantics=("arbitrary",)
    )
    x_conv, entering, final_state = pl.pallas_call(
        state_kernel,
        grid=(blocks,),
        in_specs=[
            token_block,
            fixed(8),
            fixed(8),
            pl.BlockSpec((BLOCK_LEN, STATE), lambda b: (b, 0)),
            vals_block,
            fixed(2 * LANES),
            row_block,
        ],
        out_specs=[token_block, state_block, fixed(STATE)],
        out_shape=[
            jax.ShapeDtypeStruct((tokens_here, channels), bf16),
            jax.ShapeDtypeStruct((blocks, STATE, channels), bf16),
            jax.ShapeDtypeStruct((STATE, channels), f32),
        ],
        scratch_shapes=[
            pltpu.VMEM((channels // LANES, BLOCK_LEN + 8, LANES), f32),
            pltpu.VMEM((STATE, channels), f32),
        ],
        compiler_params=limit,
        name="states",
    )(x_stream, edge_wide, taps, own_cols, vals, spread(2), per_channel(jnp.exp(totals)))

    piece = (PIECES, STATE // PIECES, channels)
    before = pl.pallas_call(
        chain_kernel,
        in_specs=[pl.BlockSpec(memory_space=pltpu.VMEM)] * 2,
        out_specs=pl.BlockSpec(memory_space=pltpu.VMEM),
        out_shape=jax.ShapeDtypeStruct((STATE, channels), bf16),
        scratch_shapes=[
            pltpu.VMEM(piece, bf16),
            pltpu.VMEM(piece, bf16),
            pltpu.SemaphoreType.DMA((PIECES,)),
            pltpu.SemaphoreType.DMA((PIECES,)),
        ],
        compiler_params=pltpu.CompilerParams(
            collective_id=0, has_side_effects=True, vmem_limit_bytes=16 * 2**20
        ),
        name="chain",
    )(final_state, per_channel(jnp.exp(jnp.sum(totals, axis=0))))

    if whole_group:
        out_specs = token_block
        out_shape = jax.ShapeDtypeStruct((tokens_here, channels), bf16)
        scratch = [pltpu.VMEM((BLOCK_LEN, channels), f32)]
    else:
        out_specs = [token_block, vals_block]
        out_shape = [
            jax.ShapeDtypeStruct((tokens_here, channels), f32),
            jax.ShapeDtypeStruct((tokens_here, LANES), f32),
        ]
        scratch = []
    result = pl.pallas_call(
        functools.partial(mix_kernel, whole_group),
        grid=(blocks,),
        in_specs=[
            token_block,
            token_block,
            pl.BlockSpec((BLOCK_LEN, 2 * STATE), lambda b: (b, 0)),
            vals_block,
            pl.BlockSpec((BLOCK_LEN, heads_here), lambda b: (b, 0)),
            pl.BlockSpec((1, heads_here, BLOCK_LEN), lambda b: (b, 0, 0)),
            state_block,
            row_block,
            fixed(STATE),
            fixed(2 * LANES),
            fixed(2 * LANES),
            fixed(1),
            fixed(1),
        ],
        out_specs=out_specs,
        out_shape=out_shape,
        scratch_shapes=scratch,
        compiler_params=limit,
        name="mix",
    )(
        x_conv, gate_z, own_cols, vals, run_scaled, run_rows, entering,
        per_channel(jnp.exp(starts)), before, spread(0), spread(1),
        per_channel(skip_d), norm_gain[None],
    )
    if whole_group:
        return result
    gated_out, squares = result
    group_total = squares[:, 0]
    for level in range(group_levels):
        group_total = group_total + swapped(group_total, "head", level)
    mean_square = group_total / (HEADS // GROUPS * head_size)
    normed = gated_out * lax.rsqrt(mean_square + 1e-05)[:, None] * norm_gain[None, :]
    return normed.astype(bf16)


def solution(mesh):
    return jax.shard_map(
        on_device,
        mesh=mesh,
        in_specs=(
            P("ctx", "head"),
            P("ctx", "head"),
            P("ctx", "head"),
            P("ctx", "head"),
            P("head"),
            P("head"),
            P("head"),
            P(None, "head"),
            P(None, "head"),
            P("head"),
        ),
        out_specs=P("ctx", "head"),
        check_vma=False,
    )
```
